512 devices in a mesh: gx: 32 (over x, z_hi, core), gy: 16 (over z_lo, y).
Axes of the slice: x: 4, y: 4, z: 16 (z_hi: 4, z_lo: 4; z = z_hi * 4 + z_lo), core: 2. Of those that a mesh axis runs over, the one named last changes fastest.
Arguments:
- coarse: bfloat16 [64, 64, 8, 256], P('gx', 'gy'), may hold values from -6 to 6
- skip: bfloat16 [128, 128, 16, 128], P('gx', 'gy'), may hold values from -6 to 6
- up_weight: bfloat16 [16384, 128], replicated, may hold values from -0.125 to 0.125
- up_bias: float32 [128], replicated, may hold values from -3 to 3
- first_weight: bfloat16 [6912, 128], replicated, may hold values from -0.078125 to 0.078125
- first_bias: float32 [128], replicated, may hold values from -3 to 3
- second_weight: bfloat16 [3456, 128], replicated, may hold values from -0.15625 to 0.15625
- second_bias: float32 [128], replicated, may hold values from -3 to 3
Outputs:
- refined: bfloat16 [128, 128, 16, 128], P('gx', 'gy')
The draws below stay inside these ranges and needn't reach their ends.
All inputs are finite; a program needn't handle non-finite values.
Results may differ from the reference program's by a relative error of at most 0.011.
Values may be sent and summed in bfloat16 or wider, within the bound.
No kernel may reach another device: no remote copies, remote signals or barrier semaphores. Data moves between devices by JAX's collectives and lax.ppermute only.
A program may use at most 64 MiB of HBM per device.

```python
import jax
import jax.numpy as jnp

CIN = 256
CF = 128
CZ = 8
CXALL = 64
CYALL = 64
FXALL = 128
FYALL = 128
FZ = 16


def block_levels(key, extent, shards, smallest, high):
    def one(position, blocks):
        steps = jax.random.uniform(jax.random.fold_in(jax.random.fold_in(key, 6), position), (blocks,), jnp.float32, smallest / len(shards), high / len(shards))
        return jnp.repeat(jnp.exp(steps), extent[position] // blocks).reshape((-1,) + (1,) * (len(extent) - position - 1))

    loudness = one(*shards[0])
    for cut in shards[1:]:
        loudness = loudness * one(*cut)
    return loudness


def scatter_about(rng, shape, width, limit, pieces=(), dtype=jnp.bfloat16):
    array = width * jax.random.normal(rng, shape, jnp.float32)
    if pieces:
        array = array * block_levels(rng, shape, pieces, -0.22, 0.18)
    return jnp.clip(array, -limit, limit).astype(dtype)


def setup_inputs(seed: int = 0) -> dict:
    streams_of = jax.random.split(jax.random.key(seed), 9)
    return {
        "coarse": scatter_about(streams_of[0], (CXALL, CYALL, CZ, CIN), 1.0, 6.0, ((0, 32), (1, 16))),
        "skip": scatter_about(streams_of[1], (FXALL, FYALL, FZ, CF), 1.0, 6.0, ((0, 32), (1, 16))),
        "up_weight": scatter_about(streams_of[2], (64 * CIN, CF), (8 * CIN) ** -0.5, 0.125),
        "up_bias": scatter_about(streams_of[3], (CF,), 0.5, 3.0, (), jnp.float32),
        "first_weight": scatter_about(streams_of[4], (54 * CF, CF), (54 * CF) ** -0.5, 0.078125),
        "first_bias": scatter_about(streams_of[5], (CF,), 0.5, 3.0, (), jnp.float32),
        "second_weight": scatter_about(streams_of[6], (27 * CF, CF), (27 * CF // 2) ** -0.5, 0.15625),
        "second_bias": scatter_about(streams_of[7], (CF,), 0.5, 3.0, (), jnp.float32),
    }


def upsample_parities(padded, weight):
    extent_x = padded.shape[0] - 2
    extent_y = padded.shape[1] - 2
    extent_z = padded.shape[2] - 2
    in_width = padded.shape[3]
    out_width = weight.shape[1]
    kernel = weight.reshape(4, 4, 4, in_width, out_width)
    taps = (((1, 0), (3, -1)), ((2, 0), (0, 1)))
    results = []
    for parity_x in range(2):
        for parity_y in range(2):
            for parity_z in range(2):
                slices = []
                weight_rows = []
                for tap_x, step_x in taps[parity_x]:
                    for tap_y, step_y in taps[parity_y]:
                        for tap_z, step_z in taps[parity_z]:
                            window = padded[1 + step_x:1 + step_x + extent_x, 1 + step_y:1 + step_y + extent_y, 1 + step_z:1 + step_z + extent_z]
                            slices.append(window.reshape(-1, in_width))
                            weight_rows.append(kernel[tap_x, tap_y, tap_z])
                product = jnp.dot(jnp.concatenate(slices, 1), jnp.concatenate(weight_rows, 0), preferred_element_type=jnp.float32)
                results.append(product.reshape(extent_x, extent_y, extent_z, out_width))
    stacked = jnp.stack(results).reshape(2, 2, 2, extent_x, extent_y, extent_z, out_width)
    stacked = stacked.transpose(3, 0, 4, 1, 5, 2, 6)
    return stacked.reshape(2 * extent_x, 2 * extent_y, 2 * extent_z, out_width)


def conv_taps(padded, weight):
    extent_x = padded.shape[0] - 2
    extent_y = padded.shape[1] - 2
    extent_z = padded.shape[2] - 2
    in_width = padded.shape[3]
    out_width = weight.shape[1]
    kernel = weight.reshape(27, in_width, out_width)
    total = jnp.zeros((extent_x * extent_y * extent_z, out_width), jnp.float32)
    for step_x in range(3):
        for step_y in range(3):
            for step_z in range(3):
                window = padded[step_x:step_x + extent_x, step_y:step_y + extent_y, step_z:step_z + extent_z]
                total = total + jnp.dot(window.reshape(-1, in_width), kernel[(step_x * 3 + step_y) * 3 + step_z], preferred_element_type=jnp.float32)
    return total.reshape(extent_x, extent_y, extent_z, out_width)


def reference(coarse, skip, up_weight, up_bias, first_weight, first_bias, second_weight, second_bias):
    border = ((1, 1), (1, 1), (1, 1), (0, 0))
    upsampled = (upsample_parities(jnp.pad(coarse, border), up_weight) + up_bias).astype(jnp.bfloat16)
    joined = jnp.concatenate([upsampled, skip], -1)
    hidden = jnp.maximum(conv_taps(jnp.pad(joined, border), first_weight) + first_bias, 0.0).astype(jnp.bfloat16)
    refined = (conv_taps(jnp.pad(hidden, border), second_weight) + second_bias).astype(jnp.bfloat16)
    return refined
```

```python
import jax
import jax.numpy as jnp
from jax import lax
from jax.experimental import pallas as pl
from jax.experimental.pallas import tpu as pltpu
from jax.sharding import PartitionSpec as P

GX = 32
GY = 16
AXES = ("gx", "gy")
BF = jnp.bfloat16
F32 = jnp.float32
VMEM = pl.BlockSpec(memory_space=pltpu.VMEM)


def rank(x, y):
    return x * GY + y


NEAR = [(rank(x, y), rank(x ^ 1, y)) for x in range(GX) for y in range(GY)]
FAR = [
    (rank(x, y), rank(((x + 1) ^ 1) - 1, y)) for x in range(1, GX - 1) for y in range(GY)
]
UP = [(rank(x, y), rank(x, y + 1)) for x in range(GX) for y in range(GY - 1)]
DOWN = [(j, i) for i, j in UP]


def send(value, pairs):
    return lax.ppermute(value, AXES, pairs)


def pack_x_kernel(coarse, skip, far, near):
    odd = lax.axis_index("gx") % 2
    for half in range(2):
        block = coarse[:, half * 128 : half * 128 + 128]
        far[half * 64 : half * 64 + 64] = block
        near[half * 64 : half * 64 + 64] = block
    far[128:384] = skip[pl.ds(2 * odd, 2)].reshape(256, 128)
    near[128:384] = skip[pl.ds(2 - 2 * odd, 2)].reshape(256, 128)


def pack_x(coarse, skip):
    edge = jax.ShapeDtypeStruct((384, 128), BF)
    return pl.pallas_call(
        pack_x_kernel,
        out_shape=(edge, edge),
        in_specs=[VMEM, VMEM],
        out_specs=(VMEM, VMEM),
    )(coarse, skip)


def pack_y_kernel(coarse, skip, near, far, up, down):
    for out, first in ((down, 0), (up, 1)):
        for half in range(2):
            for x in range(2):
                row = half * 96 + x * 16
                at = x * 32 + first * 16
                out[row : row + 16] = coarse[at : at + 16, half * 128 : half * 128 + 128]
                for s, source in ((1, near), (2, far)):
                    row = half * 96 + s * 32 + x * 16
                    at = half * 64 + x * 32 + first * 16
                    out[row : row + 16] = source[at : at + 16]
        out[192:320] = skip[:, first * 6 : first * 6 + 2].reshape(128, 128)
        for s, source in ((0, near), (1, far)):
            for x in range(2):
                row = 320 + s * 64 + x * 32
                at = 128 + x * 128 + first * 96
                out[row : row + 32] = source[at : at + 32]


def pack_y(coarse, skip, near, far):
    edge = jax.ShapeDtypeStruct((448, 128), BF)
    return pl.pallas_call(
        pack_y_kernel,
        out_shape=(edge, edge),
        in_specs=[VMEM] * 4,
        out_specs=(VMEM, VMEM),
    )(coarse, skip, near, far)


TAPS = (((1, 1), (3, 0)), ((0, 2), (2, 1)))


def later(value):
    return jnp.concatenate([jnp.zeros_like(value[:, :1]), value[:, :-1]], 1)


def earlier(value):
    return jnp.concatenate([value[:, 1:], jnp.zeros_like(value[:, :1])], 1)


def main_kernel(
    coarse, skip, near, far, low, high, uw, ub, fw, fb, sw, sb, out, cells, joined, hidden, mixed
):
    gx = lax.axis_index("gx")
    gy = lax.axis_index("gy")
    odd = gx % 2
    near_c = 4 - 4 * odd
    far_c = 4 * odd
    near_f = 6 - 6 * odd
    far_f = 6 * odd
    for half in range(2):
        lanes = slice(half * 128, half * 128 + 128)
        cells[2:4, 2:6, :, lanes] = coarse[:, lanes].astype(F32).reshape(2, 4, 8, 128)
        for at, source in ((near_c, near), (far_c, far)):
            cells[pl.ds(at, 2), 2:6, :, lanes] = (
                source[half * 64 : half * 64 + 64].astype(F32).reshape(2, 4, 8, 128)
            )
        for at, source in ((0, low), (6, high)):
            for s, x in ((0, 2), (1, near_c), (2, far_c)):
                row = half * 96 + s * 32
                cells[pl.ds(x, 2), at : at + 2, :, lanes] = (
                    source[row : row + 32].astype(F32).reshape(2, 2, 8, 128)
                )
    joined[2:6, 2:10, :, 128:256] = skip[...]
    joined[pl.ds(near_f, 2), 2:10, :, 128:256] = near[128:384].reshape(2, 8, 16, 128)
    joined[pl.ds(far_f, 2), 2:10, :, 128:256] = far[128:384].reshape(2, 8, 16, 128)
    for at, source in ((0, low), (10, high)):
        joined[2:6, at : at + 2, :, 128:256] = source[192:320].reshape(4, 2, 16, 128)
        joined[pl.ds(near_f, 2), at : at + 2, :, 128:256] = source[320:384].reshape(2, 2, 16, 128)
        joined[pl.ds(far_f, 2), at : at + 2, :, 128:256] = source[384:448].reshape(2, 2, 16, 128)
    bias = ub[...]
    for px in range(2):
        for py in range(2):
            lhs = []
            rhs = []
            for kx, ix in TAPS[px]:
                for ky, iy in TAPS[py]:
                    block = cells[ix : ix + 4, iy : iy + 6]
                    lhs.append(block.reshape(192, 256).astype(BF))
                    at = kx * 16 + ky * 4
                    rhs.append(jnp.concatenate([uw[at + kz] for kz in range(4)], 1))
            terms = jnp.dot(
                jnp.concatenate(lhs, 1), jnp.concatenate(rhs, 0), preferred_element_type=F32
            ).reshape(24, 8, 512)
            even = terms[:, :, 128:256] + later(terms[:, :, 384:512]) + bias
            uneven = terms[:, :, 256:384] + earlier(terms[:, :, 0:128]) + bias
            mixed[:, pl.ds(0, 8, 2), :] = even
            mixed[:, pl.ds(1, 8, 2), :] = uneven
            for a in range(4):
                for b in range(6):
                    joined[2 * a + px, 2 * b + py, :, 0:128] = mixed[a * 6 + b].astype(BF)

    @pl.when(gx == 0)
    def _():
        joined[0:2, :, :, 0:128] = jnp.zeros((2, 12, 16, 128), BF)

    @pl.when(gx == GX - 1)
    def _():
        joined[6:8, :, :, 0:128] = jnp.zeros((2, 12, 16, 128), BF)

    @pl.when(gy == 0)
    def _():
        joined[:, 0:2, :, 0:128] = jnp.zeros((8, 2, 16, 128), BF)

    @pl.when(gy == GY - 1)
    def _():
        joined[:, 10:12, :, 0:128] = jnp.zeros((8, 2, 16, 128), BF)

    kernel = jnp.concatenate([fw[:, dz].reshape(2304, 128) for dz in range(3)], 1)
    for x in range(0, 6, 2):
        lhs = [
            joined[x + dx : x + dx + 2, dy : dy + 10].reshape(320, 256)
            for dx in range(3)
            for dy in range(3)
        ]
        terms = jnp.dot(jnp.concatenate(lhs, 1), kernel, preferred_element_type=F32)
        terms = terms.reshape(20, 16, 384)
        value = (
            terms[:, :, 128:256]
            + later(terms[:, :, 0:128])
            + earlier(terms[:, :, 256:384])
            + fb[...]
        )
        hidden[x : x + 2] = jnp.maximum(value, 0.0).astype(BF).reshape(2, 10, 16, 128)

    @pl.when(gx == 0)
    def _():
        hidden[0:1] = jnp.zeros((1, 10, 16, 128), BF)

    @pl.when(gx == GX - 1)
    def _():
        hidden[5:6] = jnp.zeros((1, 10, 16, 128), BF)

    @pl.when(gy == 0)
    def _():
        hidden[:, 0:1] = jnp.zeros((6, 1, 16, 128), BF)

    @pl.when(gy == GY - 1)
    def _():
        hidden[:, 9:10] = jnp.zeros((6, 1, 16, 128), BF)

    kernel = jnp.concatenate([sw[:, dz].reshape(1152, 128) for dz in range(3)], 1)
    for x in range(0, 4, 2):
        lhs = [
            hidden[x + dx : x + dx + 2, dy : dy + 8].reshape(256, 128)
            for dx in range(3)
            for dy in range(3)
        ]
        terms = jnp.dot(jnp.concatenate(lhs, 1), kernel, preferred_element_type=F32)
        terms = terms.reshape(16, 16, 384)
        value = (
            terms[:, :, 128:256]
            + later(terms[:, :, 0:128])
            + earlier(terms[:, :, 256:384])
            + sb[...]
        )
        out[x : x + 2] = value.astype(BF).reshape(2, 8, 16, 128)


def main(coarse, skip, near, far, low, high, uw, ub, fw, fb, sw, sb):
    return pl.pallas_call(
        main_kernel,
        out_shape=jax.ShapeDtypeStruct((4, 8, 16, 128), BF),
        in_specs=[VMEM] * 12,
        out_specs=VMEM,
        scratch_shapes=[
            pltpu.VMEM((6, 8, 8, 256), F32),
            pltpu.VMEM((8, 12, 16, 256), BF),
            pltpu.VMEM((6, 10, 16, 128), BF),
            pltpu.VMEM((24, 16, 128), F32),
        ],
        compiler_params=pltpu.CompilerParams(vmem_limit_bytes=40 * 1024 * 1024),
        cost_estimate=pl.CostEstimate(flops=3_000_000_000, bytes_accessed=8_000_000, transcendentals=0),
    )(coarse, skip, near, far, low, high, uw, ub, fw, fb, sw, sb)


def per_device(coarse, skip, up_weight, up_bias, first_weight, first_bias, second_weight, second_bias):
    coarse = coarse.reshape(64, 256)
    far, near = pack_x(coarse, skip)
    far = send(far, FAR)
    near = send(near, NEAR)
    up, down = pack_y(coarse, skip, near, far)
    low = send(up, UP)
    high = send(down, DOWN)
    return main(
        coarse,
        skip,
        near,
        far,
        low,
        high,
        up_weight.reshape(64, 256, 128),
        up_bias.reshape(1, 128),
        first_weight.reshape(9, 3, 256, 128),
        first_bias.reshape(1, 128),
        second_weight.reshape(9, 3, 128, 128),
        second_bias.reshape(1, 128),
    )


def solution(mesh):
    return jax.shard_map(
        per_device,
        mesh=mesh,
        in_specs=(P("gx", "gy"), P("gx", "gy"), P(), P(), P(), P(), P(), P()),
        out_specs=P("gx", "gy"),
        check_vma=False,
    )
```

```python
import jax
import jax.numpy as jnp
from jax import lax
from jax.experimental import pallas as pl
from jax.experimental.pallas import tpu as pltpu
from jax.sharding import PartitionSpec as P

GX = 32
GY = 16
AXES = ("gx", "gy")
BF = jnp.bfloat16
F32 = jnp.float32
VMEM = pl.BlockSpec(memory_space=pltpu.VMEM)
HBM = pl.BlockSpec(memory_space=pltpu.HBM)
SMALL = 4 * 1024 * 1024


def in_hbm(value):
    return pltpu.with_memory_space_constraint(value, pltpu.HBM)


def in_vmem(value):
    return pltpu.VMEM(value.shape, value.dtype)


def rank(x, y):
    return x * GY + y


NEAR = [(rank(x, y), rank(x ^ 1, y)) for x in range(GX) for y in range(GY)]
FAR = [
    (rank(x, y), rank(((x + 1) ^ 1) - 1, y)) for x in range(1, GX - 1) for y in range(GY)
]
UP = [(rank(x, y), rank(x, y + 1)) for x in range(GX) for y in range(GY - 1)]
DOWN = [(j, i) for i, j in UP]


def send(value, pairs):
    return lax.ppermute(value, AXES, pairs)


def fill_x(edge, coarse, skip, first):
    for half in range(2):
        edge[half * 64 : half * 64 + 64] = coarse[:, half * 128 : half * 128 + 128]
    edge[128:384] = skip[pl.ds(first, 2)].reshape(256, 128)


def fields_kernel(coarse_in, skip_in, coarse, skip, far, sems):
    odd = lax.axis_index("gx") % 2
    copies = [
        pltpu.make_async_copy(coarse_in, coarse, sems.at[0]),
        pltpu.make_async_copy(skip_in, skip, sems.at[1]),
    ]
    for copy in copies:
        copy.start()
    for copy in copies:
        copy.wait()
    fill_x(far, coarse, skip, 2 * odd)


def fields(coarse, skip):
    return pl.pallas_call(
        fields_kernel,
        out_shape=(
            in_vmem(coarse),
            in_vmem(skip),
            pltpu.VMEM((384, 128), BF),
        ),
        in_specs=[HBM, HBM],
        out_specs=[VMEM] * 3,
        scratch_shapes=[pltpu.SemaphoreType.DMA((2,))],
        compiler_params=pltpu.CompilerParams(vmem_limit_bytes=SMALL),
    )(in_hbm(coarse), in_hbm(skip))


def stage_kernel(*refs):
    sources, coarse, skip = refs[:6], refs[6], refs[7]
    targets, near, sems = refs[8:14], refs[14], refs[15]
    odd = lax.axis_index("gx") % 2
    copies = [
        pltpu.make_async_copy(source, target, sems.at[i])
        for i, (source, target) in enumerate(zip(sources, targets))
    ]
    for copy in copies:
        copy.start()
    fill_x(near, coarse, skip, 2 - 2 * odd)
    for copy in copies:
        copy.wait()


def stage(weights, coarse, skip):
    return pl.pallas_call(
        stage_kernel,
        out_shape=[in_vmem(w) for w in weights] + [pltpu.VMEM((384, 128), BF)],
        in_specs=[HBM] * 6 + [VMEM] * 2,
        out_specs=[VMEM] * 7,
        scratch_shapes=[pltpu.SemaphoreType.DMA((6,))],
        compiler_params=pltpu.CompilerParams(vmem_limit_bytes=SMALL),
        cost_estimate=pl.CostEstimate(flops=0, bytes_accessed=14_000_000, transcendentals=0),
    )(*[in_hbm(w) for w in weights], coarse, skip)


def pack_y_kernel(coarse, skip, far, near, up, down):
    for out, first in ((down, 0), (up, 1)):
        for half in range(2):
            for x in range(2):
                row = half * 96 + x * 16
                at = x * 32 + first * 16
                out[row : row + 16] = coarse[at : at + 16, half * 128 : half * 128 + 128]
                for s, source in ((1, near), (2, far)):
                    row = half * 96 + s * 32 + x * 16
                    at = half * 64 + x * 32 + first * 16
                    out[row : row + 16] = source[at : at + 16]
        out[192:320] = skip[:, first * 6 : first * 6 + 2].reshape(128, 128)
        for s, source in ((0, near), (1, far)):
            for x in range(2):
                row = 320 + s * 64 + x * 32
                at = 128 + x * 128 + first * 96
                out[row : row + 32] = source[at : at + 32]


def pack_y(coarse, skip, far, near):
    edge = jax.ShapeDtypeStruct((448, 128), BF)
    return pl.pallas_call(
        pack_y_kernel,
        out_shape=(edge, edge),
        in_specs=[VMEM] * 4,
        out_specs=(VMEM, VMEM),
        compiler_params=pltpu.CompilerParams(vmem_limit_bytes=SMALL),
    )(coarse, skip, far, near)


TAPS = (((1, 1), (3, 0)), ((0, 2), (2, 1)))


def later(value):
    return jnp.concatenate([jnp.zeros_like(value[:, :1]), value[:, :-1]], 1)


def earlier(value):
    return jnp.concatenate([value[:, 1:], jnp.zeros_like(value[:, :1])], 1)


def main_kernel(
    coarse, skip, near, far, low, high, uw, ub, fw, fb, sw, sb, out, cells, joined, hidden, mixed
):
    gx = lax.axis_index("gx")
    gy = lax.axis_index("gy")
    odd = gx % 2
    near_c = 4 - 4 * odd
    far_c = 4 * odd
    near_f = 6 - 6 * odd
    far_f = 6 * odd
    for half in range(2):
        lanes = slice(half * 128, half * 128 + 128)
        cells[2:4, 2:6, :, lanes] = coarse[:, lanes].astype(F32).reshape(2, 4, 8, 128)
        for at, source in ((near_c, near), (far_c, far)):
            cells[pl.ds(at, 2), 2:6, :, lanes] = (
                source[half * 64 : half * 64 + 64].astype(F32).reshape(2, 4, 8, 128)
            )
        for at, source in ((0, low), (6, high)):
            for s, x in ((0, 2), (1, near_c), (2, far_c)):
                row = half * 96 + s * 32
                cells[pl.ds(x, 2), at : at + 2, :, lanes] = (
                    source[row : row + 32].astype(F32).reshape(2, 2, 8, 128)
                )
    joined[2:6, 2:10, :, 128:256] = skip[...]
    joined[pl.ds(near_f, 2), 2:10, :, 128:256] = near[128:384].reshape(2, 8, 16, 128)
    joined[pl.ds(far_f, 2), 2:10, :, 128:256] = far[128:384].reshape(2, 8, 16, 128)
    for at, source in ((0, low), (10, high)):
        joined[2:6, at : at + 2, :, 128:256] = source[192:320].reshape(4, 2, 16, 128)
        joined[pl.ds(near_f, 2), at : at + 2, :, 128:256] = source[320:384].reshape(2, 2, 16, 128)
        joined[pl.ds(far_f, 2), at : at + 2, :, 128:256] = source[384:448].reshape(2, 2, 16, 128)
    bias = ub[...]
    for px in range(2):
        for py in range(2):
            lhs = []
            rhs = []
            for kx, ix in TAPS[px]:
                for ky, iy in TAPS[py]:
                    block = cells[ix : ix + 4, iy : iy + 6]
                    lhs.append(block.reshape(192, 256).astype(BF))
                    at = kx * 16 + ky * 4
                    rhs.append(jnp.concatenate([uw[at + kz] for kz in range(4)], 1))
            terms = jnp.dot(
                jnp.concatenate(lhs, 1), jnp.concatenate(rhs, 0), preferred_element_type=F32
            ).reshape(24, 8, 512)
            even = terms[:, :, 128:256] + later(terms[:, :, 384:512]) + bias
            uneven = terms[:, :, 256:384] + earlier(terms[:, :, 0:128]) + bias
            mixed[:, pl.ds(0, 8, 2), :] = even
            mixed[:, pl.ds(1, 8, 2), :] = uneven
            for a in range(4):
                for b in range(6):
                    joined[2 * a + px, 2 * b + py, :, 0:128] = mixed[a * 6 + b].astype(BF)

    @pl.when(gx == 0)
    def _():
        joined[0:2, :, :, 0:128] = jnp.zeros((2, 12, 16, 128), BF)

    @pl.when(gx == GX - 1)
    def _():
        joined[6:8, :, :, 0:128] = jnp.zeros((2, 12, 16, 128), BF)

    @pl.when(gy == 0)
    def _():
        joined[:, 0:2, :, 0:128] = jnp.zeros((8, 2, 16, 128), BF)

    @pl.when(gy == GY - 1)
    def _():
        joined[:, 10:12, :, 0:128] = jnp.zeros((8, 2, 16, 128), BF)

    kernel = jnp.concatenate([fw[:, dz].reshape(2304, 128) for dz in range(3)], 1)
    for x in range(0, 6, 2):
        lhs = [
            joined[x + dx : x + dx + 2, dy : dy + 10].reshape(320, 256)
            for dx in range(3)
            for dy in range(3)
        ]
        terms = jnp.dot(jnp.concatenate(lhs, 1), kernel, preferred_element_type=F32)
        terms = terms.reshape(20, 16, 384)
        value = (
            terms[:, :, 128:256]
            + later(terms[:, :, 0:128])
            + earlier(terms[:, :, 256:384])
            + fb[...]
        )
        hidden[x : x + 2] = jnp.maximum(value, 0.0).astype(BF).reshape(2, 10, 16, 128)

    @pl.when(gx == 0)
    def _():
        hidden[0:1] = jnp.zeros((1, 10, 16, 128), BF)

    @pl.when(gx == GX - 1)
    def _():
        hidden[5:6] = jnp.zeros((1, 10, 16, 128), BF)

    @pl.when(gy == 0)
    def _():
        hidden[:, 0:1] = jnp.zeros((6, 1, 16, 128), BF)

    @pl.when(gy == GY - 1)
    def _():
        hidden[:, 9:10] = jnp.zeros((6, 1, 16, 128), BF)

    kernel = jnp.concatenate([sw[:, dz].reshape(1152, 128) for dz in range(3)], 1)
    for x in range(0, 4, 2):
        lhs = [
            hidden[x + dx : x + dx + 2, dy : dy + 8].reshape(256, 128)
            for dx in range(3)
            for dy in range(3)
        ]
        terms = jnp.dot(jnp.concatenate(lhs, 1), kernel, preferred_element_type=F32)
        terms = terms.reshape(16, 16, 384)
        value = (
            terms[:, :, 128:256]
            + later(terms[:, :, 0:128])
            + earlier(terms[:, :, 256:384])
            + sb[...]
        )
        out[x : x + 2] = value.astype(BF).reshape(2, 8, 16, 128)


def main(coarse, skip, near, far, low, high, uw, ub, fw, fb, sw, sb):
    return pl.pallas_call(
        main_kernel,
        out_shape=jax.ShapeDtypeStruct((4, 8, 16, 128), BF),
        in_specs=[VMEM] * 12,
        out_specs=VMEM,
        scratch_shapes=[
            pltpu.VMEM((6, 8, 8, 256), F32),
            pltpu.VMEM((8, 12, 16, 256), BF),
            pltpu.VMEM((6, 10, 16, 128), BF),
            pltpu.VMEM((24, 16, 128), F32),
        ],
        compiler_params=pltpu.CompilerParams(vmem_limit_bytes=24 * 1024 * 1024),
        cost_estimate=pl.CostEstimate(flops=3_000_000_000, bytes_accessed=8_000_000, transcendentals=0),
    )(coarse, skip, near, far, low, high, uw, ub, fw, fb, sw, sb)


def per_device(coarse, skip, up_weight, up_bias, first_weight, first_bias, second_weight, second_bias):
    coarse, skip, far = fields(coarse.reshape(64, 256), skip)
    far = send(far, FAR)
    weights = (
        up_weight.reshape(64, 256, 128),
        up_bias.reshape(1, 128),
        first_weight.reshape(9, 3, 256, 128),
        first_bias.reshape(1, 128),
        second_weight.reshape(9, 3, 128, 128),
        second_bias.reshape(1, 128),
    )
    *weights, near = stage(weights, coarse, skip)
    near = send(near, NEAR)
    up, down = pack_y(coarse, skip, far, near)
    low = send(up, UP)
    high = send(down, DOWN)
    return main(coarse, skip, near, far, low, high, *weights)


def solution(mesh):
    return jax.shard_map(
        per_device,
        mesh=mesh,
        in_specs=(P("gx", "gy"), P("gx", "gy"), P(), P(), P(), P(), P(), P()),
        out_specs=P("gx", "gy"),
        check_vma=False,
    )
```

```python
import jax
import jax.numpy as jnp
from jax import lax
from jax.experimental import pallas as pl
from jax.experimental.pallas import tpu as pltpu
from jax.sharding import PartitionSpec as P

GX = 32
GY = 16
AXES = ("gx", "gy")
BF = jnp.bfloat16
F32 = jnp.float32
VMEM = pl.BlockSpec(memory_space=pltpu.VMEM)
HBM = pl.BlockSpec(memory_space=pltpu.HBM)
ROOM = 2048
SMALL = 4 * 1024 * 1024


def in_hbm(value):
    return pltpu.with_memory_space_constraint(value, pltpu.HBM)


def in_vmem(value):
    return pltpu.VMEM(value.shape, value.dtype)


def rank(x, y):
    return x * GY + y


NEAR = [(rank(x, y), rank(x ^ 1, y)) for x in range(GX) for y in range(GY)]
FAR = [
    (rank(x, y), rank(((x + 1) ^ 1) - 1, y)) for x in range(1, GX - 1) for y in range(GY)
]
UP = [(rank(x, y), rank(x, y + 1)) for x in range(GX) for y in range(GY - 1)]
DOWN = [(j, i) for i, j in UP]


def send(value, pairs):
    return lax.ppermute(value, AXES, pairs)


def fill_x(edge, coarse, skip, first):
    for half in range(2):
        edge[half * 64 : half * 64 + 64] = coarse[:, half * 128 : half * 128 + 128]
    edge[128:384] = skip[pl.ds(first, 2)].reshape(256, 128)


def fetch(sources, targets, sems):
    copies = [
        pltpu.make_async_copy(source, target, sems.at[i])
        for i, (source, target) in enumerate(zip(sources, targets))
    ]
    for copy in copies:
        copy.start()
    return copies


def is_first():
    return (lax.axis_index("gx") // 2) % 4 == 0


def fields_kernel(*refs):
    (coarse_in, skip_in), sources, (coarse, skip, far) = refs[:2], refs[2:8], refs[8:11]
    targets, sems, weight_sems = refs[11:17], refs[17], refs[18]
    odd = lax.axis_index("gx") % 2
    for copy in fetch((coarse_in, skip_in), (coarse, skip), sems):
        copy.wait()
    fill_x(far, coarse, skip, 2 * odd)

    @pl.when(is_first())
    def _():
        for copy in fetch(sources, targets, weight_sems):
            copy.wait()


def fields(coarse, skip, weights):
    return pl.pallas_call(
        fields_kernel,
        out_shape=[in_vmem(coarse), in_vmem(skip), pltpu.VMEM((384, 128), BF)]
        + [in_vmem(w) for w in weights],
        in_specs=[HBM] * 8,
        out_specs=[VMEM] * 9,
        scratch_shapes=[pltpu.SemaphoreType.DMA((2,)), pltpu.SemaphoreType.DMA((6,))],
        compiler_params=pltpu.CompilerParams(vmem_limit_bytes=SMALL),
    )(in_hbm(coarse), in_hbm(skip), *[in_hbm(w) for w in weights])


def stage_kernel(*refs):
    sources, coarse, skip = refs[:6], refs[12], refs[13]
    targets, near, sems = refs[14:20], refs[20], refs[22]
    odd = lax.axis_index("gx") % 2
    fill_x(near, coarse, skip, 2 - 2 * odd)

    @pl.when(jnp.logical_not(is_first()))
    def _():
        for copy in fetch(sources, targets, sems):
            copy.wait()


def stage(weights, held, coarse, skip):
    return pl.pallas_call(
        stage_kernel,
        out_shape=[in_vmem(w) for w in weights] + [pltpu.VMEM((384, 128), BF), pltpu.VMEM((ROOM, 128), BF)],
        in_specs=[HBM] * 6 + [VMEM] * 8,
        out_specs=[VMEM] * 8,
        input_output_aliases={6 + i: i for i in range(6)},
        scratch_shapes=[pltpu.SemaphoreType.DMA((6,))],
        compiler_params=pltpu.CompilerParams(vmem_limit_bytes=SMALL),
        cost_estimate=pl.CostEstimate(flops=0, bytes_accessed=14_000_000, transcendentals=0),
    )(*[in_hbm(w) for w in weights], *held, coarse, skip)


def pack_y_kernel(coarse, skip, far, near, room, up, down):
    for out, first in ((down, 0), (up, 1)):
        for half in range(2):
            for x in range(2):
                row = half * 96 + x * 16
                at = x * 32 + first * 16
                out[row : row + 16] = coarse[at : at + 16, half * 128 : half * 128 + 128]
                for s, source in ((1, near), (2, far)):
                    row = half * 96 + s * 32 + x * 16
                    at = half * 64 + x * 32 + first * 16
                    out[row : row + 16] = source[at : at + 16]
        out[192:320] = skip[:, first * 6 : first * 6 + 2].reshape(128, 128)
        for s, source in ((0, near), (1, far)):
            for x in range(2):
                row = 320 + s * 64 + x * 32
                at = 128 + x * 128 + first * 96
                out[row : row + 32] = source[at : at + 32]


def pack_y(coarse, skip, far, near, room):
    edge = jax.ShapeDtypeStruct((448, 128), BF)
    return pl.pallas_call(
        pack_y_kernel,
        out_shape=(edge, edge),
        in_specs=[VMEM] * 5,
        out_specs=(VMEM, VMEM),
        compiler_params=pltpu.CompilerParams(vmem_limit_bytes=SMALL),
    )(coarse, skip, far, near, room)


TAPS = (((1, 1), (3, 0)), ((0, 2), (2, 1)))


def later(value):
    return jnp.concatenate([jnp.zeros_like(value[:, :1]), value[:, :-1]], 1)


def earlier(value):
    return jnp.concatenate([value[:, 1:], jnp.zeros_like(value[:, :1])], 1)


def upsample(cells, uw, bias, mixed, px, py, spans):
    lhs = []
    rhs = []
    for kx, ix in TAPS[px]:
        for ky, iy in TAPS[py]:
            parts = [cells[ix : ix + 4, iy + start : iy + stop] for start, stop in spans]
            block = jnp.concatenate(parts, 1) if len(parts) > 1 else parts[0]
            lhs.append(block.reshape(96, 256).astype(BF))
            at = kx * 16 + ky * 4
            rhs.append(jnp.concatenate([uw[at + kz] for kz in range(4)], 1))
    terms = jnp.dot(
        jnp.concatenate(lhs, 1), jnp.concatenate(rhs, 0), preferred_element_type=F32
    ).reshape(12, 8, 512)
    mixed[:, pl.ds(0, 8, 2), :] = terms[:, :, 128:256] + later(terms[:, :, 384:512]) + bias
    mixed[:, pl.ds(1, 8, 2), :] = terms[:, :, 256:384] + earlier(terms[:, :, 0:128]) + bias


def first_conv(joined, kernel, bias, x, count, spans):
    lhs = []
    rows = sum(stop - start for start, stop in spans)
    for dx in range(3):
        for dy in range(3):
            parts = [
                joined[x + dx : x + dx + count, start + dy : stop + dy] for start, stop in spans
            ]
            block = jnp.concatenate(parts, 1) if len(parts) > 1 else parts[0]
            lhs.append(block.reshape(count * rows * 16, 256))
    terms = jnp.dot(jnp.concatenate(lhs, 1), kernel, preferred_element_type=F32)
    terms = terms.reshape(count * rows, 16, 384)
    value = (
        terms[:, :, 128:256] + later(terms[:, :, 0:128]) + earlier(terms[:, :, 256:384]) + bias
    )
    return jnp.maximum(value, 0.0).astype(BF).reshape(count, rows, 16, 128)


def x_places():
    odd = lax.axis_index("gx") % 2
    return 4 - 4 * odd, 4 * odd, 6 - 6 * odd, 6 * odd


def inner_kernel(
    coarse, skip, near, far, uw, ub, fw, fb, upsampled, middle, cells, joined, mixed
):
    gx = lax.axis_index("gx")
    near_c, far_c, near_f, far_f = x_places()
    for half in range(2):
        lanes = slice(half * 128, half * 128 + 128)
        cells[2:4, 2:6, :, lanes] = coarse[:, lanes].astype(F32).reshape(2, 4, 8, 128)
        for at, source in ((near_c, near), (far_c, far)):
            cells[pl.ds(at, 2), 2:6, :, lanes] = (
                source[half * 64 : half * 64 + 64].astype(F32).reshape(2, 4, 8, 128)
            )
    joined[2:6, :, :, 128:256] = skip[:, 1:7]
    for at, source in ((near_f, near), (far_f, far)):
        for x in range(2):
            row = 128 + x * 128
            joined[at + x, :, :, 128:256] = source[row + 16 : row + 112].reshape(6, 16, 128)
    for px in range(2):
        for py in range(2):
            upsample(cells, uw, ub[...], mixed, px, py, ((2 - py, 5 - py),))
            for a in range(4):
                for b in range(3):
                    joined[2 * a + px, 2 * b + 1 - py, :, 0:128] = mixed[a * 3 + b].astype(BF)

    @pl.when(gx == 0)
    def _():
        joined[0:2, :, :, 0:128] = jnp.zeros((2, 6, 16, 128), BF)

    @pl.when(gx == GX - 1)
    def _():
        joined[6:8, :, :, 0:128] = jnp.zeros((2, 6, 16, 128), BF)

    upsampled[...] = joined[:, :, :, 0:128]
    kernel = jnp.concatenate([fw[:, dz].reshape(2304, 128) for dz in range(3)], 1)
    middle[...] = first_conv(joined, kernel, fb[...], 0, 6, ((0, 4),))


def inner(coarse, skip, near, far, uw, ub, fw, fb):
    return pl.pallas_call(
        inner_kernel,
        out_shape=(pltpu.VMEM((8, 6, 16, 128), BF), pltpu.VMEM((6, 4, 16, 128), BF)),
        in_specs=[VMEM] * 8,
        out_specs=(VMEM, VMEM),
        scratch_shapes=[
            pltpu.VMEM((6, 8, 8, 256), F32),
            pltpu.VMEM((8, 6, 16, 256), BF),
            pltpu.VMEM((12, 16, 128), F32),
        ],
        compiler_params=pltpu.CompilerParams(vmem_limit_bytes=16 * 1024 * 1024),
        cost_estimate=pl.CostEstimate(flops=2_500_000_000, bytes_accessed=0, transcendentals=0),
    )(coarse, skip, near, far, uw, ub, fw, fb)


def outer_kernel(
    coarse, skip, near, far, low, high, upsampled, middle, uw, ub, fw, fb, sw, sb, out,
    cells, joined, hidden, mixed,
):
    gx = lax.axis_index("gx")
    gy = lax.axis_index("gy")
    near_c, far_c, near_f, far_f = x_places()
    for half in range(2):
        lanes = slice(half * 128, half * 128 + 128)
        cells[2:4, 2:6, :, lanes] = coarse[:, lanes].astype(F32).reshape(2, 4, 8, 128)
        for at, source in ((near_c, near), (far_c, far)):
            cells[pl.ds(at, 2), 2:6, :, lanes] = (
                source[half * 64 : half * 64 + 64].astype(F32).reshape(2, 4, 8, 128)
            )
        for at, source in ((0, low), (6, high)):
            for s, x in ((0, 2), (1, near_c), (2, far_c)):
                row = half * 96 + s * 32
                cells[pl.ds(x, 2), at : at + 2, :, lanes] = (
                    source[row : row + 32].astype(F32).reshape(2, 2, 8, 128)
                )
    joined[2:6, 2:10, :, 128:256] = skip[...]
    joined[pl.ds(near_f, 2), 2:10, :, 128:256] = near[128:384].reshape(2, 8, 16, 128)
    joined[pl.ds(far_f, 2), 2:10, :, 128:256] = far[128:384].reshape(2, 8, 16, 128)
    for at, source in ((0, low), (10, high)):
        joined[2:6, at : at + 2, :, 128:256] = source[192:320].reshape(4, 2, 16, 128)
        joined[pl.ds(near_f, 2), at : at + 2, :, 128:256] = source[320:384].reshape(2, 2, 16, 128)
        joined[pl.ds(far_f, 2), at : at + 2, :, 128:256] = source[384:448].reshape(2, 2, 16, 128)
    joined[:, 3:9, :, 0:128] = upsampled[...]
    hidden[:, 3:7] = middle[...]
    for px in range(2):
        for py in range(2):
            spans = ((0, 2 - py), (5 - py, 6))
            upsample(cells, uw, ub[...], mixed, px, py, spans)
            places = [b for start, stop in spans for b in range(start, stop)]
            for a in range(4):
                for i, b in enumerate(places):
                    joined[2 * a + px, 2 * b + py, :, 0:128] = mixed[a * 3 + i].astype(BF)

    @pl.when(gx == 0)
    def _():
        joined[0:2, :, :, 0:128] = jnp.zeros((2, 12, 16, 128), BF)

    @pl.when(gx == GX - 1)
    def _():
        joined[6:8, :, :, 0:128] = jnp.zeros((2, 12, 16, 128), BF)

    @pl.when(gy == 0)
    def _():
        joined[:, 0:2, :, 0:128] = jnp.zeros((8, 2, 16, 128), BF)

    @pl.when(gy == GY - 1)
    def _():
        joined[:, 10:12, :, 0:128] = jnp.zeros((8, 2, 16, 128), BF)

    kernel = jnp.concatenate([fw[:, dz].reshape(2304, 128) for dz in range(3)], 1)
    for x in (0, 3):
        value = first_conv(joined, kernel, fb[...], x, 3, ((0, 3), (7, 10)))
        hidden[x : x + 3, 0:3] = value[:, 0:3]
        hidden[x : x + 3, 7:10] = value[:, 3:6]

    @pl.when(gx == 0)
    def _():
        hidden[0:1] = jnp.zeros((1, 10, 16, 128), BF)

    @pl.when(gx == GX - 1)
    def _():
        hidden[5:6] = jnp.zeros((1, 10, 16, 128), BF)

    @pl.when(gy == 0)
    def _():
        hidden[:, 0:1] = jnp.zeros((6, 1, 16, 128), BF)

    @pl.when(gy == GY - 1)
    def _():
        hidden[:, 9:10] = jnp.zeros((6, 1, 16, 128), BF)

    kernel = jnp.concatenate([sw[:, dz].reshape(1152, 128) for dz in range(3)], 1)
    for x in range(0, 4, 2):
        lhs = [
            hidden[x + dx : x + dx + 2, dy : dy + 8].reshape(256, 128)
            for dx in range(3)
            for dy in range(3)
        ]
        terms = jnp.dot(jnp.concatenate(lhs, 1), kernel, preferred_element_type=F32)
        terms = terms.reshape(16, 16, 384)
        value = (
            terms[:, :, 128:256]
            + later(terms[:, :, 0:128])
            + earlier(terms[:, :, 256:384])
            + sb[...]
        )
        out[x : x + 2] = value.astype(BF).reshape(2, 8, 16, 128)


def outer(coarse, skip, near, far, low, high, upsampled, middle, *weights):
    return pl.pallas_call(
        outer_kernel,
        out_shape=jax.ShapeDtypeStruct((4, 8, 16, 128), BF),
        in_specs=[VMEM] * 14,
        out_specs=VMEM,
        scratch_shapes=[
            pltpu.VMEM((6, 8, 8, 256), F32),
            pltpu.VMEM((8, 12, 16, 256), BF),
            pltpu.VMEM((6, 10, 16, 128), BF),
            pltpu.VMEM((12, 16, 128), F32),
        ],
        compiler_params=pltpu.CompilerParams(vmem_limit_bytes=24 * 1024 * 1024),
        cost_estimate=pl.CostEstimate(flops=3_000_000_000, bytes_accessed=0, transcendentals=0),
    )(coarse, skip, near, far, low, high, upsampled, middle, *weights)


def per_device(coarse, skip, up_weight, up_bias, first_weight, first_bias, second_weight, second_bias):
    weights = (
        up_weight.reshape(64, 256, 128),
        up_bias.reshape(1, 128),
        first_weight.reshape(9, 3, 256, 128),
        first_bias.reshape(1, 128),
        second_weight.reshape(9, 3, 128, 128),
        second_bias.reshape(1, 128),
    )
    coarse, skip, far, *held = fields(coarse.reshape(64, 256), skip, weights)
    far = send(far, FAR)
    *weights, near, room = stage(weights, held, coarse, skip)
    near = send(near, NEAR)
    up, down = pack_y(coarse, skip, far, near, room)
    low = send(up, UP)
    high = send(down, DOWN)
    upsampled, middle = inner(coarse, skip, near, far, *weights[:4])
    return outer(coarse, skip, near, far, low, high, upsampled, middle, *weights)


def solution(mesh):
    return jax.shard_map(
        per_device,
        mesh=mesh,
        in_specs=(P("gx", "gy"), P("gx", "gy"), P(), P(), P(), P(), P(), P()),
        out_specs=P("gx", "gy"),
        check_vma=False,
    )
```

```python
import jax
import jax.numpy as jnp
from jax import lax
from jax.experimental import pallas as pl
from jax.experimental.pallas import tpu as pltpu
from jax.sharding import PartitionSpec as P

GX = 32
GY = 16
AXES = ("gx", "gy")
BF = jnp.bfloat16
F32 = jnp.float32
VMEM = pl.BlockSpec(memory_space=pltpu.VMEM)
HBM = pl.BlockSpec(memory_space=pltpu.HBM)
ROOM = 2048
SMALL = 4 * 1024 * 1024


def in_hbm(value):
    return pltpu.with_memory_space_constraint(value, pltpu.HBM)


def in_vmem(value):
    return pltpu.VMEM(value.shape, value.dtype)


def rank(x, y):
    return x * GY + y


NEAR = [(rank(x, y), rank(x ^ 1, y)) for x in range(GX) for y in range(GY)]
FAR = [
    (rank(x, y), rank(((x + 1) ^ 1) - 1, y)) for x in range(1, GX - 1) for y in range(GY)
]
UP = [(rank(x, y), rank(x, y + 1)) for x in range(GX) for y in range(GY - 1)]
DOWN = [(j, i) for i, j in UP]


def send(value, pairs):
    return lax.ppermute(value, AXES, pairs)


def fill_x(edge, coarse, skip, first):
    for half in range(2):
        edge[half * 64 : half * 64 + 64] = coarse[:, half * 128 : half * 128 + 128]
    edge[128:384] = skip[pl.ds(first, 2)].reshape(256, 128)


def fetch(sources, targets, sems):
    copies = [
        pltpu.make_async_copy(source, target, sems.at[i])
        for i, (source, target) in enumerate(zip(sources, targets))
    ]
    for copy in copies:
        copy.start()
    return copies


def is_first():
    return (lax.axis_index("gx") // 2) % 4 == 0


def fields_kernel(*refs):
    (coarse_in, skip_in), sources, (coarse, skip, far) = refs[:2], refs[2:8], refs[8:11]
    targets, sems, weight_sems = refs[11:17], refs[17], refs[18]
    odd = lax.axis_index("gx") % 2
    for copy in fetch((coarse_in, skip_in), (coarse, skip), sems):
        copy.wait()
    fill_x(far, coarse, skip, 2 * odd)

    @pl.when(is_first())
    def _():
        for copy in fetch(sources, targets, weight_sems):
            copy.wait()


def fields(coarse, skip, weights):
    return pl.pallas_call(
        fields_kernel,
        out_shape=[in_vmem(coarse), in_vmem(skip), pltpu.VMEM((384, 128), BF)]
        + [in_vmem(w) for w in weights],
        in_specs=[HBM] * 8,
        out_specs=[VMEM] * 9,
        scratch_shapes=[pltpu.SemaphoreType.DMA((2,)), pltpu.SemaphoreType.DMA((6,))],
        compiler_params=pltpu.CompilerParams(vmem_limit_bytes=SMALL),
    )(in_hbm(coarse), in_hbm(skip), *[in_hbm(w) for w in weights])


def stage_kernel(*refs):
    sources, coarse, skip = refs[:6], refs[12], refs[13]
    targets, near, sems = refs[14:20], refs[20], refs[22]
    odd = lax.axis_index("gx") % 2
    fill_x(near, coarse, skip, 2 - 2 * odd)

    @pl.when(jnp.logical_not(is_first()))
    def _():
        for copy in fetch(sources, targets, sems):
            copy.wait()


def stage(weights, held, coarse, skip):
    return pl.pallas_call(
        stage_kernel,
        out_shape=[in_vmem(w) for w in weights] + [pltpu.VMEM((384, 128), BF), pltpu.VMEM((ROOM, 128), BF)],
        in_specs=[HBM] * 6 + [VMEM] * 8,
        out_specs=[VMEM] * 8,
        input_output_aliases={6 + i: i for i in range(6)},
        scratch_shapes=[pltpu.SemaphoreType.DMA((6,))],
        compiler_params=pltpu.CompilerParams(vmem_limit_bytes=SMALL),
        cost_estimate=pl.CostEstimate(flops=0, bytes_accessed=14_000_000, transcendentals=0),
    )(*[in_hbm(w) for w in weights], *held, coarse, skip)


def pack_y_kernel(coarse, skip, far, near, room, up, down):
    for out, first in ((down, 0), (up, 1)):
        for half in range(2):
            for x in range(2):
                row = half * 96 + x * 16
                at = x * 32 + first * 16
                out[row : row + 16] = coarse[at : at + 16, half * 128 : half * 128 + 128]
                for s, source in ((1, near), (2, far)):
                    row = half * 96 + s * 32 + x * 16
                    at = half * 64 + x * 32 + first * 16
                    out[row : row + 16] = source[at : at + 16]
        out[192:320] = skip[:, first * 6 : first * 6 + 2].reshape(128, 128)
        for s, source in ((0, near), (1, far)):
            for x in range(2):
                row = 320 + s * 64 + x * 32
                at = 128 + x * 128 + first * 96
                out[row : row + 32] = source[at : at + 32]


def pack_y(coarse, skip, far, near, room):
    edge = jax.ShapeDtypeStruct((448, 128), BF)
    return pl.pallas_call(
        pack_y_kernel,
        out_shape=(edge, edge),
        in_specs=[VMEM] * 5,
        out_specs=(VMEM, VMEM),
        compiler_params=pltpu.CompilerParams(vmem_limit_bytes=SMALL),
    )(coarse, skip, far, near, room)


TAPS = (((1, 1), (3, 0)), ((0, 2), (2, 1)))


def later(value):
    return jnp.concatenate([jnp.zeros_like(value[:, :1]), value[:, :-1]], 1)


def earlier(value):
    return jnp.concatenate([value[:, 1:], jnp.zeros_like(value[:, :1])], 1)


def upsample(cells, uw, bias, mixed, px, py, spans):
    lhs = []
    rhs = []
    for kx, ix in TAPS[px]:
        for ky, iy in TAPS[py]:
            parts = [cells[ix : ix + 4, iy + start : iy + stop] for start, stop in spans]
            block = jnp.concatenate(parts, 1) if len(parts) > 1 else parts[0]
            lhs.append(block.reshape(96, 256).astype(BF))
            at = kx * 16 + ky * 4
            rhs.append(jnp.concatenate([uw[at + kz] for kz in range(4)], 1))
    terms = jnp.dot(
        jnp.concatenate(lhs, 1), jnp.concatenate(rhs, 0), preferred_element_type=F32
    ).reshape(12, 8, 512)
    mixed[:, pl.ds(0, 8, 2), :] = terms[:, :, 128:256] + later(terms[:, :, 384:512]) + bias
    mixed[:, pl.ds(1, 8, 2), :] = terms[:, :, 256:384] + earlier(terms[:, :, 0:128]) + bias


def taps_side_by_side(weight, depth):
    return jnp.concatenate([weight[:, dz].reshape(9 * depth, 128) for dz in range(3)], 1)


def conv(field, kernel, bias, x, count, spans):
    depth = field.shape[3]
    lhs = []
    rows = sum(stop - start for start, stop in spans)
    for dx in range(3):
        for dy in range(3):
            parts = [field[x + dx : x + dx + count, start + dy : stop + dy] for start, stop in spans]
            block = jnp.concatenate(parts, 1) if len(parts) > 1 else parts[0]
            lhs.append(block.reshape(count * rows * 16, depth))
    terms = jnp.dot(jnp.concatenate(lhs, 1), kernel, preferred_element_type=F32)
    terms = terms.reshape(count * rows, 16, 384)
    value = (
        terms[:, :, 128:256] + later(terms[:, :, 0:128]) + earlier(terms[:, :, 256:384]) + bias
    )
    return value.reshape(count, rows, 16, 128)


def row_terms(field, kernel, x, count, spans):
    lhs = []
    rows = sum(stop - start for start, stop in spans)
    for dx in range(3):
        parts = [field[x + dx : x + dx + count, start:stop] for start, stop in spans]
        block = jnp.concatenate(parts, 1) if len(parts) > 1 else parts[0]
        lhs.append(block.reshape(count * rows * 16, 256))
    terms = jnp.dot(jnp.concatenate(lhs, 1), kernel, preferred_element_type=F32)
    return terms.reshape(count, rows, 16, 384)


def row_kernels(weight):
    return [
        jnp.concatenate(
            [
                jnp.concatenate([weight[3 * dx + dy, dz] for dz in range(3)], 1)
                for dx in range(3)
            ],
            0,
        )
        for dy in range(3)
    ]


def along_z(terms):
    count, rows = terms.shape[:2]
    terms = terms.reshape(count * rows, 16, 384)
    value = terms[:, :, 128:256] + later(terms[:, :, 0:128]) + earlier(terms[:, :, 256:384])
    return value.reshape(count, rows, 16, 128)


def rectified(value):
    return jnp.maximum(value, 0.0).astype(BF)


def x_places():
    odd = lax.axis_index("gx") % 2
    return 4 - 4 * odd, 4 * odd, 6 - 6 * odd, 6 * odd


def inner_kernel(
    coarse, skip, near, far, uw, ub, fw, fb, sw, sb, upsampled, middle, core, begun, cells, joined, mixed
):
    gx = lax.axis_index("gx")
    near_c, far_c, near_f, far_f = x_places()
    for half in range(2):
        lanes = slice(half * 128, half * 128 + 128)
        cells[2:4, 2:6, :, lanes] = coarse[:, lanes].astype(F32).reshape(2, 4, 8, 128)
        for at, source in ((near_c, near), (far_c, far)):
            cells[pl.ds(at, 2), 2:6, :, lanes] = (
                source[half * 64 : half * 64 + 64].astype(F32).reshape(2, 4, 8, 128)
            )
    joined[2:6, :, :, 128:256] = skip[:, 1:7]
    for at, source in ((near_f, near), (far_f, far)):
        for x in range(2):
            row = 128 + x * 128
            joined[at + x, :, :, 128:256] = source[row + 16 : row + 112].reshape(6, 16, 128)
    for px in range(2):
        for py in range(2):
            upsample(cells, uw, ub[...], mixed, px, py, ((2 - py, 5 - py),))
            for a in range(4):
                for b in range(3):
                    joined[2 * a + px, 2 * b + 1 - py, :, 0:128] = mixed[a * 3 + b].astype(BF)

    @pl.when(gx == 0)
    def _():
        joined[0:2, :, :, 0:128] = jnp.zeros((2, 6, 16, 128), BF)

    @pl.when(gx == GX - 1)
    def _():
        joined[6:8, :, :, 0:128] = jnp.zeros((2, 6, 16, 128), BF)

    upsampled[...] = joined[:, :, :, 0:128]
    kernel = taps_side_by_side(fw, 256)
    middle[...] = rectified(conv(joined, kernel, fb[...], 0, 6, ((0, 4),)))

    @pl.when(gx == 0)
    def _():
        middle[0:1] = jnp.zeros((1, 4, 16, 128), BF)

    @pl.when(gx == GX - 1)
    def _():
        middle[5:6] = jnp.zeros((1, 4, 16, 128), BF)

    kernels = row_kernels(fw)
    below = row_terms(joined, kernels[0], 0, 6, ((4, 6),))
    level = row_terms(joined, kernels[1], 0, 6, ((0, 1), (5, 6)))
    above = row_terms(joined, kernels[2], 0, 6, ((0, 2),))
    begun[...] = along_z(
        jnp.concatenate(
            [
                above[:, 0:1],
                above[:, 1:2] + level[:, 0:1],
                below[:, 0:1] + level[:, 1:2],
                below[:, 1:2],
            ],
            1,
        )
    )
    core[...] = conv(middle, taps_side_by_side(sw, 128), sb[...], 0, 4, ((0, 2),)).astype(BF)


def inner(coarse, skip, near, far, *weights):
    return pl.pallas_call(
        inner_kernel,
        out_shape=(
            pltpu.VMEM((8, 6, 16, 128), BF),
            pltpu.VMEM((6, 4, 16, 128), BF),
            pltpu.VMEM((4, 2, 16, 128), BF),
            pltpu.VMEM((6, 4, 16, 128), F32),
        ),
        in_specs=[VMEM] * 10,
        out_specs=[VMEM] * 4,
        scratch_shapes=[
            pltpu.VMEM((6, 8, 8, 256), F32),
            pltpu.VMEM((8, 6, 16, 256), BF),
            pltpu.VMEM((12, 16, 128), F32),
        ],
        compiler_params=pltpu.CompilerParams(vmem_limit_bytes=16 * 1024 * 1024),
        cost_estimate=pl.CostEstimate(flops=2_500_000_000, bytes_accessed=0, transcendentals=0),
    )(coarse, skip, near, far, *weights)


def outer_kernel(
    coarse, skip, near, far, low, high, upsampled, middle, core, begun, uw, ub, fw, fb, sw, sb, out,
    cells, joined, hidden, mixed, result, sems,
):
    gx = lax.axis_index("gx")
    gy = lax.axis_index("gy")
    near_c, far_c, near_f, far_f = x_places()
    for half in range(2):
        lanes = slice(half * 128, half * 128 + 128)
        cells[2:4, 2:6, :, lanes] = coarse[:, lanes].astype(F32).reshape(2, 4, 8, 128)
        for at, source in ((near_c, near), (far_c, far)):
            cells[pl.ds(at, 2), 2:6, :, lanes] = (
                source[half * 64 : half * 64 + 64].astype(F32).reshape(2, 4, 8, 128)
            )
        for at, source in ((0, low), (6, high)):
            for s, x in ((0, 2), (1, near_c), (2, far_c)):
                row = half * 96 + s * 32
                cells[pl.ds(x, 2), at : at + 2, :, lanes] = (
                    source[row : row + 32].astype(F32).reshape(2, 2, 8, 128)
                )
    joined[2:6, 2:10, :, 128:256] = skip[...]
    joined[pl.ds(near_f, 2), 2:10, :, 128:256] = near[128:384].reshape(2, 8, 16, 128)
    joined[pl.ds(far_f, 2), 2:10, :, 128:256] = far[128:384].reshape(2, 8, 16, 128)
    for at, source in ((0, low), (10, high)):
        joined[2:6, at : at + 2, :, 128:256] = source[192:320].reshape(4, 2, 16, 128)
        joined[pl.ds(near_f, 2), at : at + 2, :, 128:256] = source[320:384].reshape(2, 2, 16, 128)
        joined[pl.ds(far_f, 2), at : at + 2, :, 128:256] = source[384:448].reshape(2, 2, 16, 128)
    joined[:, 3:9, :, 0:128] = upsampled[...]
    hidden[:, 3:7] = middle[...]
    result[:, 3:5] = core[...]
    for px in range(2):
        for py in range(2):
            spans = ((0, 2 - py), (5 - py, 6))
            upsample(cells, uw, ub[...], mixed, px, py, spans)
            places = [b for start, stop in spans for b in range(start, stop)]
            for a in range(4):
                for i, b in enumerate(places):
                    joined[2 * a + px, 2 * b + py, :, 0:128] = mixed[a * 3 + i].astype(BF)

    @pl.when(gx == 0)
    def _():
        joined[0:2, :, :, 0:128] = jnp.zeros((2, 12, 16, 128), BF)

    @pl.when(gx == GX - 1)
    def _():
        joined[6:8, :, :, 0:128] = jnp.zeros((2, 12, 16, 128), BF)

    @pl.when(gy == 0)
    def _():
        joined[:, 0:2, :, 0:128] = jnp.zeros((8, 2, 16, 128), BF)

    @pl.when(gy == GY - 1)
    def _():
        joined[:, 10:12, :, 0:128] = jnp.zeros((8, 2, 16, 128), BF)

    kernels = row_kernels(fw)
    for x in (0, 3):
        below = row_terms(joined, kernels[0], x, 3, ((0, 3), (9, 10)))
        level = row_terms(joined, kernels[1], x, 3, ((1, 3), (9, 11)))
        above = row_terms(joined, kernels[2], x, 3, ((2, 3), (9, 12)))
        value = along_z(
            jnp.concatenate(
                [
                    below[:, 0:1] + level[:, 0:1] + above[:, 0:1],
                    below[:, 1:2] + level[:, 1:2],
                    below[:, 2:3],
                    above[:, 1:2],
                    level[:, 2:3] + above[:, 2:3],
                    below[:, 3:4] + level[:, 3:4] + above[:, 3:4],
                ],
                1,
            )
        )
        started = begun[x : x + 3]
        hidden[x : x + 3, 0:1] = rectified(value[:, 0:1] + fb[...])
        hidden[x : x + 3, 1:3] = rectified(value[:, 1:3] + started[:, 0:2] + fb[...])
        hidden[x : x + 3, 7:9] = rectified(value[:, 3:5] + started[:, 2:4] + fb[...])
        hidden[x : x + 3, 9:10] = rectified(value[:, 5:6] + fb[...])

    @pl.when(gx == 0)
    def _():
        hidden[0:1] = jnp.zeros((1, 10, 16, 128), BF)

    @pl.when(gx == GX - 1)
    def _():
        hidden[5:6] = jnp.zeros((1, 10, 16, 128), BF)

    @pl.when(gy == 0)
    def _():
        hidden[:, 0:1] = jnp.zeros((6, 1, 16, 128), BF)

    @pl.when(gy == GY - 1)
    def _():
        hidden[:, 9:10] = jnp.zeros((6, 1, 16, 128), BF)

    kernel = taps_side_by_side(sw, 128)
    copies = []
    for half in range(2):
        x = 2 * half
        value = conv(hidden, kernel, sb[...], x, 2, ((0, 3), (5, 8))).astype(BF)
        result[x : x + 2, 0:3] = value[:, 0:3]
        result[x : x + 2, 5:8] = value[:, 3:6]
        copy = pltpu.make_async_copy(
            result.at[x : x + 2], out.at[x : x + 2], sems.at[half]
        )
        copy.start()
        copies.append(copy)
    for copy in copies:
        copy.wait()


def outer(coarse, skip, near, far, low, high, upsampled, middle, core, begun, *weights):
    return pl.pallas_call(
        outer_kernel,
        out_shape=pltpu.HBM((4, 8, 16, 128), BF),
        in_specs=[VMEM] * 16,
        out_specs=HBM,
        scratch_shapes=[
            pltpu.VMEM((6, 8, 8, 256), F32),
            pltpu.VMEM((8, 12, 16, 256), BF),
            pltpu.VMEM((6, 10, 16, 128), BF),
            pltpu.VMEM((12, 16, 128), F32),
            pltpu.VMEM((4, 8, 16, 128), BF),
            pltpu.SemaphoreType.DMA((2,)),
        ],
        compiler_params=pltpu.CompilerParams(vmem_limit_bytes=24 * 1024 * 1024),
        cost_estimate=pl.CostEstimate(flops=3_000_000_000, bytes_accessed=0, transcendentals=0),
    )(coarse, skip, near, far, low, high, upsampled, middle, core, begun, *weights)


def per_device(coarse, skip, up_weight, up_bias, first_weight, first_bias, second_weight, second_bias):
    weights = (
        up_weight.reshape(64, 256, 128),
        up_bias.reshape(1, 128),
        first_weight.reshape(9, 3, 256, 128),
        first_bias.reshape(1, 128),
        second_weight.reshape(9, 3, 128, 128),
        second_bias.reshape(1, 128),
    )
    coarse, skip, far, *held = fields(coarse.reshape(64, 256), skip, weights)
    far = send(far, FAR)
    *weights, near, room = stage(weights, held, coarse, skip)
    near = send(near, NEAR)
    up, down = pack_y(coarse, skip, far, near, room)
    low = send(up, UP)
    high = send(down, DOWN)
    upsampled, middle, core, begun = inner(coarse, skip, near, far, *weights)
    return outer(coarse, skip, near, far, low, high, upsampled, middle, core, begun, *weights)


def solution(mesh):
    return jax.shard_map(
        per_device,
        mesh=mesh,
        in_specs=(P("gx", "gy"), P("gx", "gy"), P(), P(), P(), P(), P(), P()),
        out_specs=P("gx", "gy"),
        check_vma=False,
    )
```

```python
import jax
import jax.numpy as jnp
from jax import lax
from jax.experimental import pallas as pl
from jax.experimental.pallas import tpu as pltpu
from jax.sharding import PartitionSpec as P

GX = 32
GY = 16
AXES = ("gx", "gy")
BF = jnp.bfloat16
F32 = jnp.float32
VMEM = pl.BlockSpec(memory_space=pltpu.VMEM)
HBM = pl.BlockSpec(memory_space=pltpu.HBM)
ROOM = 2048
SMALL = 4 * 1024 * 1024


def in_hbm(value):
    return pltpu.with_memory_space_constraint(value, pltpu.HBM)


def in_vmem(value):
    return pltpu.VMEM(value.shape, value.dtype)


def rank(x, y):
    return x * GY + y


NEAR = [(rank(x, y), rank(x ^ 1, y)) for x in range(GX) for y in range(GY)]
FAR = [
    (rank(x, y), rank(((x + 1) ^ 1) - 1, y)) for x in range(1, GX - 1) for y in range(GY)
]
UP = [(rank(x, y), rank(x, y + 1)) for x in range(GX) for y in range(GY - 1)]
DOWN = [(j, i) for i, j in UP]


def send(value, pairs):
    return lax.ppermute(value, AXES, pairs)


def fill_x(edge, coarse, skip, first):
    for half in range(2):
        edge[half * 64 : half * 64 + 64] = coarse[:, half * 128 : half * 128 + 128]
    edge[128:384] = skip[pl.ds(first, 2)].reshape(256, 128)


def fetch(sources, targets, sems):
    copies = [
        pltpu.make_async_copy(source, target, sems.at[i])
        for i, (source, target) in enumerate(zip(sources, targets))
    ]
    for copy in copies:
        copy.start()
    return copies


def is_first():
    return (lax.axis_index("gx") // 2) % 4 == 0


def fields_kernel(*refs):
    (coarse_in, skip_in), sources, (coarse, skip, far) = refs[:2], refs[2:8], refs[8:11]
    targets, sems, weight_sems = refs[11:17], refs[17], refs[18]
    odd = lax.axis_index("gx") % 2
    for copy in fetch((coarse_in, skip_in), (coarse, skip), sems):
        copy.wait()
    fill_x(far, coarse, skip, 2 * odd)

    @pl.when(is_first())
    def _():
        for copy in fetch(sources, targets, weight_sems):
            copy.wait()


def fields(coarse, skip, weights):
    return pl.pallas_call(
        fields_kernel,
        out_shape=[in_vmem(coarse), in_vmem(skip), pltpu.VMEM((384, 128), BF)]
        + [in_vmem(w) for w in weights],
        in_specs=[HBM] * 8,
        out_specs=[VMEM] * 9,
        scratch_shapes=[pltpu.SemaphoreType.DMA((2,)), pltpu.SemaphoreType.DMA((6,))],
        compiler_params=pltpu.CompilerParams(vmem_limit_bytes=SMALL),
    )(in_hbm(coarse), in_hbm(skip), *[in_hbm(w) for w in weights])


def stage_kernel(*refs):
    sources, coarse, skip = refs[:6], refs[12], refs[13]
    targets, near, sems = refs[14:20], refs[20], refs[22]
    odd = lax.axis_index("gx") % 2
    fill_x(near, coarse, skip, 2 - 2 * odd)

    @pl.when(jnp.logical_not(is_first()))
    def _():
        for copy in fetch(sources, targets, sems):
            copy.wait()


def stage(weights, held, coarse, skip):
    return pl.pallas_call(
        stage_kernel,
        out_shape=[in_vmem(w) for w in weights] + [pltpu.VMEM((384, 128), BF), pltpu.VMEM((ROOM, 128), BF)],
        in_specs=[HBM] * 6 + [VMEM] * 8,
        out_specs=[VMEM] * 8,
        input_output_aliases={6 + i: i for i in range(6)},
        scratch_shapes=[pltpu.SemaphoreType.DMA((6,))],
        compiler_params=pltpu.CompilerParams(vmem_limit_bytes=SMALL),
        cost_estimate=pl.CostEstimate(flops=0, bytes_accessed=14_000_000, transcendentals=0),
    )(*[in_hbm(w) for w in weights], *held, coarse, skip)


def pack_y_kernel(coarse, skip, far, near, room, up, down):
    for out, first in ((down, 0), (up, 1)):
        for half in range(2):
            for x in range(2):
                row = half * 96 + x * 16
                at = x * 32 + first * 16
                out[row : row + 16] = coarse[at : at + 16, half * 128 : half * 128 + 128]
                for s, source in ((1, near), (2, far)):
                    row = half * 96 + s * 32 + x * 16
                    at = half * 64 + x * 32 + first * 16
                    out[row : row + 16] = source[at : at + 16]
        out[192:320] = skip[:, first * 6 : first * 6 + 2].reshape(128, 128)
        for s, source in ((0, near), (1, far)):
            for x in range(2):
                row = 320 + s * 64 + x * 32
                at = 128 + x * 128 + first * 96
                out[row : row + 32] = source[at : at + 32]


def pack_y(coarse, skip, far, near, room):
    edge = jax.ShapeDtypeStruct((448, 128), BF)
    return pl.pallas_call(
        pack_y_kernel,
        out_shape=(edge, edge),
        in_specs=[VMEM] * 5,
        out_specs=(VMEM, VMEM),
        compiler_params=pltpu.CompilerParams(vmem_limit_bytes=SMALL),
    )(coarse, skip, far, near, room)


TAPS = (((1, 1), (3, 0)), ((0, 2), (2, 1)))


def later(value):
    return jnp.concatenate([jnp.zeros_like(value[:, :1]), value[:, :-1]], 1)


def earlier(value):
    return jnp.concatenate([value[:, 1:], jnp.zeros_like(value[:, :1])], 1)


def upsample(cells, uw, bias, mixed, px, py, spans):
    lhs = []
    rhs = []
    for kx, ix in TAPS[px]:
        for ky, iy in TAPS[py]:
            parts = [cells[ix : ix + 4, iy + start : iy + stop] for start, stop in spans]
            block = jnp.concatenate(parts, 1) if len(parts) > 1 else parts[0]
            lhs.append(block.reshape(96, 256).astype(BF))
            at = kx * 16 + ky * 4
            rhs.append(jnp.concatenate([uw[at + kz] for kz in range(4)], 1))
    terms = jnp.dot(
        jnp.concatenate(lhs, 1), jnp.concatenate(rhs, 0), preferred_element_type=F32
    ).reshape(12, 8, 512)
    mixed[:, pl.ds(0, 8, 2), :] = terms[:, :, 128:256] + later(terms[:, :, 384:512]) + bias
    mixed[:, pl.ds(1, 8, 2), :] = terms[:, :, 256:384] + earlier(terms[:, :, 0:128]) + bias


def taps_side_by_side(weight, depth):
    return jnp.concatenate([weight[:, dz].reshape(9 * depth, 128) for dz in range(3)], 1)


def conv(field, kernel, bias, x, count, spans):
    depth = field.shape[3]
    lhs = []
    rows = sum(stop - start for start, stop in spans)
    for dx in range(3):
        for dy in range(3):
            parts = [field[x + dx : x + dx + count, start + dy : stop + dy] for start, stop in spans]
            block = jnp.concatenate(parts, 1) if len(parts) > 1 else parts[0]
            lhs.append(block.reshape(count * rows * 16, depth))
    terms = jnp.dot(jnp.concatenate(lhs, 1), kernel, preferred_element_type=F32)
    terms = terms.reshape(count * rows, 16, 384)
    value = (
        terms[:, :, 128:256] + later(terms[:, :, 0:128]) + earlier(terms[:, :, 256:384]) + bias
    )
    return value.reshape(count, rows, 16, 128)


def row_terms(field, kernel, x, count, spans):
    lhs = []
    rows = sum(stop - start for start, stop in spans)
    for dx in range(3):
        parts = [field[x + dx : x + dx + count, start:stop] for start, stop in spans]
        block = jnp.concatenate(parts, 1) if len(parts) > 1 else parts[0]
        lhs.append(block.reshape(count * rows * 16, field.shape[3]))
    terms = jnp.dot(jnp.concatenate(lhs, 1), kernel, preferred_element_type=F32)
    return terms.reshape(count, rows, 16, 384)


def row_kernels(weight):
    return [
        jnp.concatenate(
            [
                jnp.concatenate([weight[3 * dx + dy, dz] for dz in range(3)], 1)
                for dx in range(3)
            ],
            0,
        )
        for dy in range(3)
    ]


def along_z(terms):
    count, rows = terms.shape[:2]
    terms = terms.reshape(count * rows, 16, 384)
    value = terms[:, :, 128:256] + later(terms[:, :, 0:128]) + earlier(terms[:, :, 256:384])
    return value.reshape(count, rows, 16, 128)


def rectified(value):
    return jnp.maximum(value, 0.0).astype(BF)


def x_places():
    odd = lax.axis_index("gx") % 2
    return 4 - 4 * odd, 4 * odd, 6 - 6 * odd, 6 * odd


def inner_kernel(
    coarse, skip, near, far, uw, ub, fw, fb, sw, sb, upsampled, middle, core, begun, begun_out, cells, joined, mixed
):
    gx = lax.axis_index("gx")
    near_c, far_c, near_f, far_f = x_places()
    for half in range(2):
        lanes = slice(half * 128, half * 128 + 128)
        cells[2:4, 2:6, :, lanes] = coarse[:, lanes].astype(F32).reshape(2, 4, 8, 128)
        for at, source in ((near_c, near), (far_c, far)):
            cells[pl.ds(at, 2), 2:6, :, lanes] = (
                source[half * 64 : half * 64 + 64].astype(F32).reshape(2, 4, 8, 128)
            )
    joined[2:6, :, :, 128:256] = skip[:, 1:7]
    for at, source in ((near_f, near), (far_f, far)):
        for x in range(2):
            row = 128 + x * 128
            joined[at + x, :, :, 128:256] = source[row + 16 : row + 112].reshape(6, 16, 128)
    for px in range(2):
        for py in range(2):
            upsample(cells, uw, ub[...], mixed, px, py, ((2 - py, 5 - py),))
            for a in range(4):
                for b in range(3):
                    joined[2 * a + px, 2 * b + 1 - py, :, 0:128] = mixed[a * 3 + b].astype(BF)

    @pl.when(gx == 0)
    def _():
        joined[0:2, :, :, 0:128] = jnp.zeros((2, 6, 16, 128), BF)

    @pl.when(gx == GX - 1)
    def _():
        joined[6:8, :, :, 0:128] = jnp.zeros((2, 6, 16, 128), BF)

    upsampled[...] = joined[:, :, :, 0:128]
    kernel = taps_side_by_side(fw, 256)
    middle[...] = rectified(conv(joined, kernel, fb[...], 0, 6, ((0, 4),)))

    @pl.when(gx == 0)
    def _():
        middle[0:1] = jnp.zeros((1, 4, 16, 128), BF)

    @pl.when(gx == GX - 1)
    def _():
        middle[5:6] = jnp.zeros((1, 4, 16, 128), BF)

    kernels = row_kernels(fw)
    below = row_terms(joined, kernels[0], 0, 6, ((4, 6),))
    level = row_terms(joined, kernels[1], 0, 6, ((0, 1), (5, 6)))
    above = row_terms(joined, kernels[2], 0, 6, ((0, 2),))
    begun[...] = along_z(
        jnp.concatenate(
            [
                above[:, 0:1],
                above[:, 1:2] + level[:, 0:1],
                below[:, 0:1] + level[:, 1:2],
                below[:, 1:2],
            ],
            1,
        )
    )
    kernels = row_kernels(sw)
    below = row_terms(middle, kernels[0], 0, 4, ((2, 4),))
    level = row_terms(middle, kernels[1], 0, 4, ((0, 1), (3, 4)))
    above = row_terms(middle, kernels[2], 0, 4, ((0, 2),))
    begun_out[...] = along_z(
        jnp.concatenate(
            [
                above[:, 0:1],
                above[:, 1:2] + level[:, 0:1],
                below[:, 0:1] + level[:, 1:2],
                below[:, 1:2],
            ],
            1,
        )
    )
    core[...] = conv(middle, taps_side_by_side(sw, 128), sb[...], 0, 4, ((0, 2),)).astype(BF)


def inner(coarse, skip, near, far, *weights):
    return pl.pallas_call(
        inner_kernel,
        out_shape=(
            pltpu.VMEM((8, 6, 16, 128), BF),
            pltpu.VMEM((6, 4, 16, 128), BF),
            pltpu.VMEM((4, 2, 16, 128), BF),
            pltpu.VMEM((6, 4, 16, 128), F32),
            pltpu.VMEM((4, 4, 16, 128), F32),
        ),
        in_specs=[VMEM] * 10,
        out_specs=[VMEM] * 5,
        scratch_shapes=[
            pltpu.VMEM((6, 8, 8, 256), F32),
            pltpu.VMEM((8, 6, 16, 256), BF),
            pltpu.VMEM((12, 16, 128), F32),
        ],
        compiler_params=pltpu.CompilerParams(vmem_limit_bytes=16 * 1024 * 1024),
        cost_estimate=pl.CostEstimate(flops=2_500_000_000, bytes_accessed=0, transcendentals=0),
    )(coarse, skip, near, far, *weights)


def outer_kernel(
    coarse, skip, near, far, low, high, upsampled, middle, core, begun, begun_out, uw, ub, fw, fb, sw, sb, out,
    cells, joined, hidden, mixed, result, sems,
):
    gx = lax.axis_index("gx")
    gy = lax.axis_index("gy")
    near_c, far_c, near_f, far_f = x_places()
    for half in range(2):
        lanes = slice(half * 128, half * 128 + 128)
        cells[2:4, 2:6, :, lanes] = coarse[:, lanes].astype(F32).reshape(2, 4, 8, 128)
        for at, source in ((near_c, near), (far_c, far)):
            cells[pl.ds(at, 2), 2:6, :, lanes] = (
                source[half * 64 : half * 64 + 64].astype(F32).reshape(2, 4, 8, 128)
            )
        for at, source in ((0, low), (6, high)):
            for s, x in ((0, 2), (1, near_c), (2, far_c)):
                row = half * 96 + s * 32
                cells[pl.ds(x, 2), at : at + 2, :, lanes] = (
                    source[row : row + 32].astype(F32).reshape(2, 2, 8, 128)
                )
    joined[2:6, 2:10, :, 128:256] = skip[...]
    joined[pl.ds(near_f, 2), 2:10, :, 128:256] = near[128:384].reshape(2, 8, 16, 128)
    joined[pl.ds(far_f, 2), 2:10, :, 128:256] = far[128:384].reshape(2, 8, 16, 128)
    for at, source in ((0, low), (10, high)):
        joined[2:6, at : at + 2, :, 128:256] = source[192:320].reshape(4, 2, 16, 128)
        joined[pl.ds(near_f, 2), at : at + 2, :, 128:256] = source[320:384].reshape(2, 2, 16, 128)
        joined[pl.ds(far_f, 2), at : at + 2, :, 128:256] = source[384:448].reshape(2, 2, 16, 128)
    joined[:, 3:9, :, 0:128] = upsampled[...]
    hidden[:, 3:7] = middle[...]
    result[:, 3:5] = core[...]
    for px in range(2):
        for py in range(2):
            spans = ((0, 2 - py), (5 - py, 6))
            upsample(cells, uw, ub[...], mixed, px, py, spans)
            places = [b for start, stop in spans for b in range(start, stop)]
            for a in range(4):
                for i, b in enumerate(places):
                    joined[2 * a + px, 2 * b + py, :, 0:128] = mixed[a * 3 + i].astype(BF)

    @pl.when(gx == 0)
    def _():
        joined[0:2, :, :, 0:128] = jnp.zeros((2, 12, 16, 128), BF)

    @pl.when(gx == GX - 1)
    def _():
        joined[6:8, :, :, 0:128] = jnp.zeros((2, 12, 16, 128), BF)

    @pl.when(gy == 0)
    def _():
        joined[:, 0:2, :, 0:128] = jnp.zeros((8, 2, 16, 128), BF)

    @pl.when(gy == GY - 1)
    def _():
        joined[:, 10:12, :, 0:128] = jnp.zeros((8, 2, 16, 128), BF)

    kernels = row_kernels(fw)
    for x in (0, 3):
        below = row_terms(joined, kernels[0], x, 3, ((0, 3), (9, 10)))
        level = row_terms(joined, kernels[1], x, 3, ((1, 3), (9, 11)))
        above = row_terms(joined, kernels[2], x, 3, ((2, 3), (9, 12)))
        value = along_z(
            jnp.concatenate(
                [
                    below[:, 0:1] + level[:, 0:1] + above[:, 0:1],
                    below[:, 1:2] + level[:, 1:2],
                    below[:, 2:3],
                    above[:, 1:2],
                    level[:, 2:3] + above[:, 2:3],
                    below[:, 3:4] + level[:, 3:4] + above[:, 3:4],
                ],
                1,
            )
        )
        started = begun[x : x + 3]
        hidden[x : x + 3, 0:1] = rectified(value[:, 0:1] + fb[...])
        hidden[x : x + 3, 1:3] = rectified(value[:, 1:3] + started[:, 0:2] + fb[...])
        hidden[x : x + 3, 7:9] = rectified(value[:, 3:5] + started[:, 2:4] + fb[...])
        hidden[x : x + 3, 9:10] = rectified(value[:, 5:6] + fb[...])

    @pl.when(gx == 0)
    def _():
        hidden[0:1] = jnp.zeros((1, 10, 16, 128), BF)

    @pl.when(gx == GX - 1)
    def _():
        hidden[5:6] = jnp.zeros((1, 10, 16, 128), BF)

    @pl.when(gy == 0)
    def _():
        hidden[:, 0:1] = jnp.zeros((6, 1, 16, 128), BF)

    @pl.when(gy == GY - 1)
    def _():
        hidden[:, 9:10] = jnp.zeros((6, 1, 16, 128), BF)

    kernels = row_kernels(sw)
    copies = []
    for half in range(2):
        x = 2 * half
        below = row_terms(hidden, kernels[0], x, 2, ((0, 3), (7, 8)))
        level = row_terms(hidden, kernels[1], x, 2, ((1, 3), (7, 9)))
        above = row_terms(hidden, kernels[2], x, 2, ((2, 3), (7, 10)))
        value = along_z(
            jnp.concatenate(
                [
                    below[:, 0:1] + level[:, 0:1] + above[:, 0:1],
                    below[:, 1:2] + level[:, 1:2],
                    below[:, 2:3],
                    above[:, 1:2],
                    level[:, 2:3] + above[:, 2:3],
                    below[:, 3:4] + level[:, 3:4] + above[:, 3:4],
                ],
                1,
            )
        )
        started = begun_out[x : x + 2]
        result[x : x + 2, 0:1] = (value[:, 0:1] + sb[...]).astype(BF)
        result[x : x + 2, 1:3] = (value[:, 1:3] + started[:, 0:2] + sb[...]).astype(BF)
        result[x : x + 2, 5:7] = (value[:, 3:5] + started[:, 2:4] + sb[...]).astype(BF)
        result[x : x + 2, 7:8] = (value[:, 5:6] + sb[...]).astype(BF)
        copy = pltpu.make_async_copy(
            result.at[x : x + 2], out.at[x : x + 2], sems.at[half]
        )
        copy.start()
        copies.append(copy)
    for copy in copies:
        copy.wait()


def outer(coarse, skip, near, far, low, high, upsampled, middle, core, begun, begun_out, *weights):
    return pl.pallas_call(
        outer_kernel,
        out_shape=pltpu.HBM((4, 8, 16, 128), BF),
        in_specs=[VMEM] * 17,
        out_specs=HBM,
        scratch_shapes=[
            pltpu.VMEM((6, 8, 8, 256), F32),
            pltpu.VMEM((8, 12, 16, 256), BF),
            pltpu.VMEM((6, 10, 16, 128), BF),
            pltpu.VMEM((12, 16, 128), F32),
            pltpu.VMEM((4, 8, 16, 128), BF),
            pltpu.SemaphoreType.DMA((2,)),
        ],
        compiler_params=pltpu.CompilerParams(vmem_limit_bytes=24 * 1024 * 1024),
        cost_estimate=pl.CostEstimate(flops=3_000_000_000, bytes_accessed=0, transcendentals=0),
    )(coarse, skip, near, far, low, high, upsampled, middle, core, begun, begun_out, *weights)


def per_device(coarse, skip, up_weight, up_bias, first_weight, first_bias, second_weight, second_bias):
    weights = (
        up_weight.reshape(64, 256, 128),
        up_bias.reshape(1, 128),
        first_weight.reshape(9, 3, 256, 128),
        first_bias.reshape(1, 128),
        second_weight.reshape(9, 3, 128, 128),
        second_bias.reshape(1, 128),
    )
    coarse, skip, far, *held = fields(coarse.reshape(64, 256), skip, weights)
    far = send(far, FAR)
    *weights, near, room = stage(weights, held, coarse, skip)
    near = send(near, NEAR)
    up, down = pack_y(coarse, skip, far, near, room)
    low = send(up, UP)
    high = send(down, DOWN)
    upsampled, middle, core, begun, begun_out = inner(coarse, skip, near, far, *weights)
    return outer(coarse, skip, near, far, low, high, upsampled, middle, core, begun, begun_out, *weights)


def solution(mesh):
    return jax.shard_map(
        per_device,
        mesh=mesh,
        in_specs=(P("gx", "gy"), P("gx", "gy"), P(), P(), P(), P(), P(), P()),
        out_specs=P("gx", "gy"),
        check_vma=False,
    )
```
